32 devices in a mesh: sec: 2 (over core), section: 4 (over z), expert: 4 (over y, x).
Axes of the slice: x: 2, y: 2, z: 4, core: 2. Of those that a mesh axis runs over, the one named last changes fastest.
Arguments:
- tokens: bfloat16 [512, 2048], P('expert', ('sec', 'section')), may hold values from -6 to 6
- cotangent: bfloat16 [512, 2048], P('expert', ('sec', 'section')), may hold values from -6 to 6
- expert_ids: int32 [512, 2], P('expert'), may hold values from 0 to 3, all different within a row; in each aligned block of 128 rows (0 to 127, 128 to 255, ...) at most 96 rows name the same one
- gate_values: float32 [512, 2], P('expert'), may hold values from 0.2 to 1
- expand_weight: bfloat16 [4, 2048, 4096], P('expert', None, ('sec', 'section')), may hold values from -0.125 to 0.125
- contract_weight: bfloat16 [4, 4096, 2048], P('expert', ('sec', 'section')), may hold values from -0.09375 to 0.09375
Outputs:
- combined: bfloat16 [512, 2048], P('expert', ('sec', 'section'))
- input_grad: bfloat16 [512, 2048], P('expert', ('sec', 'section'))
- gate_grad: float32 [512, 2], P('expert')
The draws below stay inside these ranges and needn't reach their ends.
Inputs may be any that keep to these rules, and one draw needn't show every extreme that they name: `expert_ids`: the two ids of a token differ. Among the 128 tokens of one index of expert, no expert is named by more than 96 of them, a bound that some block reaches.
All inputs are finite; a program needn't handle non-finite values.
Results may differ from the reference program's by a relative error of at most 0.015.
Values may be sent and summed in bfloat16 or wider, within the bound.
A program may use at most 64 MiB of HBM per device.

```python
import math
from functools import partial
import jax
import jax.numpy as jnp
import numpy as np
from jax import lax

D = 2048
FF = 4096
TOK_DEV = 128
EXPERTS = 4
TOKENS = 512
CAP = 96
N_SEC = 2
N_SECTION = 4
N_EXPERT = 4


def levels(rng, extent, cuts, smallest, largest):
    def one(axis_at, blocks):
        steps = jax.random.uniform(jax.random.fold_in(jax.random.fold_in(rng, 6), axis_at), (blocks,), jnp.float32, smallest / len(cuts), largest / len(cuts))
        return jnp.repeat(jnp.exp(steps), extent[axis_at] // blocks).reshape((-1,) + (1,) * (len(extent) - axis_at - 1))

    gain = one(*cuts[0])
    for cut in cuts[1:]:
        gain = gain * one(*cut)
    return gain


def routed_block(rng, own, number, rows, number_of, top, bound, lean):
    order = jax.random.permutation(rng, number_of)
    crowded, usual = portions_of(number_of, rows * top, bound, lean, True), portions_of(number_of, rows * top, bound, lean, False)
    places = jnp.arange(number_of)

    def named(tallies, turn):
        used = int((tallies > 0).sum())
        fixed = max(1, used // 4)
        moved = fixed + (places - fixed + turn * (used - fixed)) % max(1, number_of - fixed)
        return jnp.zeros((number_of,), jnp.int32).at[order[jnp.where(places < fixed, places, moved)]].set(jnp.asarray(tallies, jnp.int32))

    tallies = jnp.where(number % 4 == 0, named(crowded, number // 4), named(usual, number - number // 4 - 1))
    mixed = jax.random.permutation(jax.random.fold_in(own, 3), number_of)
    source_of, receiver = mixed[0:number_of // 2 * 2:2], mixed[1:number_of // 2 * 2:2]
    room = jnp.minimum(tallies[source_of] - 1, bound - tallies[receiver]) // 2
    room = jnp.where((source_of == order[0]) | (receiver == order[0]) | (tallies[receiver] == 0), 0, jnp.maximum(room, 0))
    moved = jax.random.randint(jax.random.fold_in(own, 4), (number_of // 2,), 0, 1 << 20) % (room + 1)
    tallies = tallies.at[source_of].add(-moved).at[receiver].add(moved)
    members = jnp.searchsorted(jnp.cumsum(tallies), jnp.arange(rows * top), side="right").astype(jnp.int32)
    listing = members.reshape(top, rows).T
    listing = listing[jax.random.permutation(jax.random.fold_in(own, 1), rows)]
    turn = jax.random.randint(jax.random.fold_in(own, 2), (rows, 1), 0, top)
    return jnp.take_along_axis(listing, (jnp.arange(top)[None, :] + turn) % top, axis=1)


def portions_of(count, total, reach, lean, full):
    weights = [(1 << 20) // math.isqrt(standing ** lean) + 1 for standing in range(1, count + 1)]
    largest = reach if full else min(reach, max(-(-total // count), total * weights[0] // sum(weights)))
    least = 1 if total - largest >= count - 1 else 0
    counts, surplus = [largest] + [least] * (count - 1), total - largest - least * (count - 1)
    while surplus > 0:
        free = [i for i in range(1, count) if counts[i] < largest] or [i for i in range(1, count) if counts[i] < reach]
        mass, left = sum([weights[i] for i in free]), surplus
        for i in free:
            more = min(reach - counts[i], max(1, left * weights[i] // mass), surplus)
            counts[i] = counts[i] + more
            surplus = surplus - more
    return np.array(counts)


def scatter_about(rng, shape, width, most, cuts=(), kind=jnp.bfloat16):
    result = width * jax.random.normal(rng, shape, jnp.float32)
    if cuts:
        result = result * levels(rng, shape, cuts, -0.22, 0.18)
    return jnp.clip(result, -most, most).astype(kind)


def setup_inputs(seed: int = 0) -> dict:
    seeds = jax.random.split(jax.random.key(seed), 7)
    tokens = scatter_about(seeds[0], (TOKENS, D), 1.0, 6.0, ((0, 4), (1, 8)))
    cotangent = scatter_about(seeds[1], (TOKENS, D), 1.0, 6.0, ((0, 4), (1, 8)))
    expert_ids_keys = jax.random.split(jax.random.fold_in(seeds[2], 1), TOKENS // TOK_DEV)
    expert_ids_turns = jax.random.permutation(jax.random.fold_in(seeds[2], 3), TOKENS // TOK_DEV)
    expert_ids = jax.vmap(lambda own, number: routed_block(jax.random.fold_in(seeds[2], 2), own, number, TOK_DEV, EXPERTS, 2, CAP, 2))(expert_ids_keys, expert_ids_turns).reshape((TOKENS, 2))
    gate_values = jnp.clip(0.2 + 0.8 * jax.random.uniform(seeds[3], (TOKENS, 2), jnp.float32) ** levels(seeds[3], (TOKENS, 2), ((0, 4),), -0.2, 0.2), 0.2, 1.0)
    expand_weight = scatter_about(seeds[4], (EXPERTS, D, FF), D ** -0.5, 0.125, ((0, 4), (2, 8)))
    contract_weight = scatter_about(seeds[5], (EXPERTS, FF, D), FF ** -0.5, 0.09375, ((0, 4), (1, 8)))
    return {"tokens": tokens, "cotangent": cotangent, "expert_ids": expert_ids, "gate_values": gate_values, "expand_weight": expand_weight, "contract_weight": contract_weight}


gelu_coef = math.sqrt(2.0 / math.pi)
gelu_cubic = 0.044715

def gelu_parts(hidden):
    inner_arg = gelu_coef * (hidden + gelu_cubic * hidden * hidden * hidden)
    tanh_value = jnp.tanh(inner_arg)
    activation = 0.5 * hidden * (1.0 + tanh_value)
    derivative = 0.5 * (1.0 + tanh_value) + 0.5 * hidden * (1.0 - tanh_value * tanh_value) * gelu_coef * (1.0 + 3.0 * gelu_cubic * hidden * hidden)
    return (activation, derivative)

def slot_positions(expert_ids, capacity, experts):
    flat_ids = expert_ids.reshape(-1).astype(jnp.int32)
    one_hot = (flat_ids[:, None] == jnp.arange(experts, dtype=jnp.int32)[None, :]).astype(jnp.int32)
    earlier = lax.optimization_barrier(jnp.sum((jnp.cumsum(one_hot, axis=0) - one_hot) * one_hot, axis=1))
    return (flat_ids * capacity + earlier).astype(jnp.int32)

def reference(tokens, cotangent, expert_ids, gate_values, expand_weight, contract_weight):
    blocks = N_SEC * N_SECTION
    share = FF // blocks
    slot_count = N_EXPERT * CAP
    grouped = expert_ids.reshape(N_EXPERT, TOK_DEV, 2)
    positions = jax.vmap(partial(slot_positions, capacity=CAP, experts=EXPERTS))(grouped)
    source = jnp.arange(N_EXPERT, dtype=jnp.int32)[:, None]
    target_rows = (positions // CAP * slot_count + source * CAP + positions % CAP).astype(jnp.int32).reshape(-1)
    pairs_x = jnp.broadcast_to(tokens[:, None, :], (TOKENS, 2, D)).reshape(TOKENS * 2, D)
    scaled_grad = (gate_values[:, :, None] * cotangent[:, None, :].astype(jnp.float32)).astype(jnp.bfloat16)
    pairs_g = scaled_grad.reshape(TOKENS * 2, D)
    buffer_x = jnp.zeros((EXPERTS * slot_count, D), jnp.bfloat16).at[target_rows].set(pairs_x).reshape(EXPERTS, slot_count, D)
    buffer_g = jnp.zeros((EXPERTS * slot_count, D), jnp.bfloat16).at[target_rows].set(pairs_g).reshape(EXPERTS, slot_count, D)

    def expert_step(packed):
        rows_x, rows_g, w_expand, w_contract = packed
        hidden = jnp.dot(rows_x, w_expand, preferred_element_type=jnp.float32)
        activation, derivative = gelu_parts(hidden)
        activation = activation.astype(jnp.bfloat16)
        grad_activation = jnp.dot(rows_g, w_contract.T, preferred_element_type=jnp.float32)
        grad_hidden = (grad_activation * derivative).astype(jnp.bfloat16)
        act_blocks = activation.astype(jnp.float32).reshape(slot_count, blocks, share)
        contract_blocks = w_contract.astype(jnp.float32).reshape(blocks, share, D)
        out_terms = jnp.einsum('rbf,bfd->brd', act_blocks, contract_blocks).astype(jnp.bfloat16)
        out_terms = lax.optimization_barrier(out_terms).astype(jnp.float32)
        expert_out = lax.optimization_barrier(jnp.sum(out_terms, axis=0)).astype(jnp.bfloat16)
        grad_blocks = grad_hidden.astype(jnp.float32).reshape(slot_count, blocks, share)
        expand_blocks = w_expand.astype(jnp.float32).reshape(D, blocks, share)
        back_terms = jnp.einsum('rbf,dbf->brd', grad_blocks, expand_blocks).astype(jnp.bfloat16)
        back_terms = lax.optimization_barrier(back_terms).astype(jnp.float32)
        expert_back = lax.optimization_barrier(jnp.sum(back_terms, axis=0)).astype(jnp.bfloat16)
        return (expert_out, expert_back)
    outputs, backs = lax.map(expert_step, (buffer_x, buffer_g, expand_weight, contract_weight))
    out_pairs = outputs.reshape(EXPERTS * slot_count, D)[target_rows].astype(jnp.float32).reshape(TOKENS, 2, D)
    back_pairs = backs.reshape(EXPERTS * slot_count, D)[target_rows].astype(jnp.float32).reshape(TOKENS, 2, D)
    combined = lax.optimization_barrier(jnp.sum(gate_values[:, :, None] * out_pairs, axis=1)).astype(jnp.bfloat16)
    gate_grad = lax.optimization_barrier(jnp.sum(cotangent[:, None, :].astype(jnp.float32) * out_pairs, axis=2))
    input_grad = lax.optimization_barrier(jnp.sum(back_pairs, axis=1)).astype(jnp.bfloat16)
    return (combined, input_grad, gate_grad)
```

```python
import math

import jax
import jax.numpy as jnp
from jax import lax
from jax.experimental import pallas as pl
from jax.experimental.pallas import tpu as pltpu
from jax.sharding import PartitionSpec as P

MESH = pl.DeviceIdType.MESH
F32 = jnp.float32
BF16 = jnp.bfloat16


def partners(i):
    return (i, i + 1 - 2 * lax.rem(i, 2), lax.rem(i + 2, 4), 3 - i)


def kernel(
    tok, cot, ids, gate, w1_hbm, w2_hbm,
    comb_out, grad_out, gg_out,
    w1, w2, zbuf, sendbuf, slots, pt, gslot, pmat, pgate, hid, gact, act, ghid,
    own, sibs, sibr, rsend, ret, xsend, xret, gbuf, zs2, zr2, keep,
    wsem, zsend, zrecv, asend, arecv, fsend, frecv, bsend, brecv,
    rs_send, rs_recv, x_send, x_recv, g_send, g_recv, q_send, q_recv,
):
    cap = slots.shape[4]
    wd = slots.shape[5]
    tr = tok.shape[0]
    rows = 4 * cap
    c = lax.axis_index("sec")
    z = lax.axis_index("section")
    e = lax.axis_index("expert")
    zp = partners(z)
    ep = partners(e)

    def to_z(s):
        return {"section": zp[s]}

    def to_e(d):
        return {"expert": ep[d]}

    sib = {"sec": 1 - c}

    def rcopy(src, dst, ss, rs, dev):
        return pltpu.make_async_remote_copy(
            src_ref=src, dst_ref=dst, send_sem=ss, recv_sem=rs,
            device_id=dev, device_id_type=MESH,
        )

    cw1 = pltpu.make_async_copy(w1_hbm.at[0], w1, wsem.at[0])
    cw2 = pltpu.make_async_copy(w2_hbm.at[0], w2, wsem.at[1])
    cw1.start()
    cw2.start()

    zbuf[0, 0] = tok[...]
    zbuf[0, 1] = cot[...]
    barrier = pltpu.get_barrier_semaphore()
    peers = [to_z(s) for s in (1, 2, 3)] + [to_e(d) for d in (1, 2, 3)] + [sib]
    peers += [{"section": zp[s], "sec": 1 - c} for s in (1, 2, 3)]
    for p in peers:
        pl.semaphore_signal(barrier, inc=1, device_id=p, device_id_type=MESH)
    pl.semaphore_wait(barrier, len(peers))

    sends = []
    zc = {}
    for s in (1, 2, 3):
        zc[s] = rcopy(zbuf.at[0], zbuf.at[s], zsend.at[s], zrecv.at[s], to_z(s))
        zc[s].start()
        sends.append(zc[s])

    rid = lax.broadcasted_iota(jnp.int32, (8, tr), 0)
    erow = jnp.where(rid == 0, ep[0], jnp.where(rid == 1, ep[1], jnp.where(rid == 2, ep[2], jnp.where(rid == 3, ep[3], -1))))
    is0 = ids[0:1, :] == erow
    is1 = ids[1:2, :] == erow
    named = jnp.where(is0, 1.0, jnp.where(is1, 1.0, 0.0)).astype(F32)
    gates = jnp.where(is0, gate[0:1, :], jnp.where(is1, gate[1:2, :], 0.0))
    upper = (
        lax.broadcasted_iota(jnp.int32, (tr, tr), 0) < lax.broadcasted_iota(jnp.int32, (tr, tr), 1)
    ).astype(F32).astype(BF16)
    rank = jnp.dot(named.astype(BF16), upper, preferred_element_type=F32)
    key = jnp.where(named > 0.5, rank, -1.0).astype(jnp.int32)
    cid = lax.broadcasted_iota(jnp.int32, (cap, tr), 0)
    for d in range(4):
        hit = cid == key[d : d + 1, :]
        one = jnp.where(hit, 1.0, 0.0).astype(F32)
        weighed = jnp.where(hit, gates[d : d + 1, :], 0.0)
        pt[d] = one.astype(BF16)
        gslot[d] = jnp.broadcast_to(jnp.sum(weighed, axis=1, keepdims=True), (cap, wd))
        own[0, 0, d * cap : (d + 1) * cap, 0:tr] = one
        own[0, 1, d * cap : (d + 1) * cap, 0:tr] = weighed
    pmat[...] = own[0, 0, :, 0:tr].T.astype(BF16)
    pgate[...] = own[0, 1, :, 0:tr].T.astype(BF16)

    cw1.wait()
    cw2.wait()

    def block(core, s):
        return pl.ds(pl.multiple_of((core * 4 + zp[s]) * wd, wd), wd)

    def gather_step(half, core, s, first):
        at = block(core, s)
        xs = slots[half, s, :, 0].reshape(rows, wd)
        gs = slots[half, s, :, 1].reshape(rows, wd)
        hpart = jnp.dot(xs, w1[at, :], preferred_element_type=F32)
        gpart = lax.dot_general(gs, w2[:, at], (((1,), (1,)), ((), ())), preferred_element_type=F32)
        if first:
            hid[...] = hpart
            gact[...] = gpart
        else:
            hid[...] += hpart
            gact[...] += gpart

    ac = {}
    fc = {}

    def dispatch(s):
        if s:
            zc[s].wait_recv()
        xb = zbuf[s, 0]
        cb = zbuf[s, 1]
        for d in (3, 1, 2, 0):
            dst = slots.at[0, s, 0] if d == 0 else sendbuf.at[s, d]
            dst[0] = jnp.dot(pt[d], xb, preferred_element_type=F32).astype(BF16)
            dst[1] = (jnp.dot(pt[d], cb, preferred_element_type=F32) * gslot[d]).astype(BF16)
            if d:
                ac[s, d] = rcopy(sendbuf.at[s, d], slots.at[0, s, d], asend.at[s, d], arecv.at[s, d], to_e(d))
                ac[s, d].start()
                sends.append(ac[s, d])

    def take(s):
        for d in (1, 2, 3):
            ac[s, d].wait_recv()
        fc[s] = rcopy(slots.at[0, s], slots.at[1, s], fsend.at[s], frecv.at[s], sib)
        fc[s].start()
        sends.append(fc[s])
        gather_step(0, c, s, s == 0)

    def take_sib(s):
        fc[s].wait_recv()
        gather_step(1, 1 - c, s, False)

    dispatch(0)
    dispatch(1)
    take(0)
    dispatch(2)
    take(1)
    take_sib(0)
    dispatch(3)
    take(2)
    take_sib(1)
    take(3)
    take_sib(2)
    take_sib(3)

    coef = math.sqrt(2.0 / math.pi)
    cubic = 0.044715
    lane = lax.broadcasted_iota(jnp.int32, (cap, 128), 1)
    xc = {}
    for d in (3, 1, 2, 0):
        rr = slice(d * cap, (d + 1) * cap)
        h = hid[rr, :]
        ga = gact[rr, :]
        h2 = h * h
        u = jnp.tanh(coef * h * (1.0 + cubic * h2))
        half = 0.5 * (1.0 + u)
        a = (h * half).astype(BF16)
        act[rr, :] = a
        ghid[rr, :] = (ga * (half + 0.5 * h * (1.0 - u * u) * coef * (1.0 + 3.0 * cubic * h2))).astype(BF16)
        dots = jnp.sum(a.astype(F32) * ga, axis=1, keepdims=True)
        hi = dots.astype(BF16).astype(F32)
        lo = dots - hi
        extra = jnp.where(lane == 2 * d, hi, jnp.where(lane == 2 * d + 1, lo, 0.0)).astype(BF16)
        if d:
            xsend[d] = extra
            xc[d] = rcopy(xsend.at[d], xret.at[d], x_send.at[d], x_recv.at[d], to_e(d))
            xc[d].start()
            sends.append(xc[d])
        else:
            xret[0] = extra

    bc = {}
    rc = {}
    qc = {}

    def expand_back(s):
        for core, mine in ((1 - c, False), (c, True)):
            at = block(core, s)
            o = jnp.dot(act[...], w2[:, at], preferred_element_type=F32)
            b = lax.dot_general(ghid[...], w1[at, :], (((1,), (1,)), ((), ())), preferred_element_type=F32)
            if mine:
                own[s, 0] = o
                own[s, 1] = b
            else:
                sibs[s, 0] = o.astype(BF16)
                sibs[s, 1] = b.astype(BF16)
                bc[s] = rcopy(sibs.at[s], sibr.at[s], bsend.at[s], brecv.at[s], sib)
                bc[s].start()
                sends.append(bc[s])

    def give_back(s):
        bc[s].wait_recv()
        for d in (3, 1, 2, 0):
            rr = slice(d * cap, (d + 1) * cap)
            dst = ret.at[s, 0] if d == 0 else rsend.at[s, d]
            for k in range(2):
                dst[k] = (own[s, k, rr, :] + sibr[s, k, rr, :].astype(F32)).astype(BF16)
            if d:
                rc[s, d] = rcopy(rsend.at[s, d], ret.at[s, d], rs_send.at[s, d], rs_recv.at[s, d], to_e(d))
                rc[s, d].start()
                sends.append(rc[s, d])

    def join(s):
        for d in (1, 2, 3):
            rc[s, d].wait_recv()
        o = jnp.dot(pgate[...], ret[s, :, 0].reshape(rows, wd), preferred_element_type=F32)
        b = jnp.dot(pmat[...], ret[s, :, 1].reshape(rows, wd), preferred_element_type=F32)
        if s:
            zs2[s, 0] = o.astype(BF16)
            zs2[s, 1] = b.astype(BF16)
            qc[s] = rcopy(zs2.at[s], zr2.at[s], q_send.at[s], q_recv.at[s], to_z(s))
            qc[s].start()
            sends.append(qc[s])
        else:
            keep[0] = o
            keep[1] = b

    expand_back(3)
    expand_back(2)
    give_back(3)
    expand_back(1)
    give_back(2)
    expand_back(0)
    give_back(1)
    give_back(0)

    for d in (1, 2, 3):
        xc[d].wait_recv()
    share = jnp.dot(pmat[...], xret[...].reshape(rows, 128), preferred_element_type=F32)
    gbuf[0] = share.T[0:8, :]
    gc = []
    for i, dev in enumerate([to_z(1), to_z(2), to_z(3), sib] + [{"section": zp[s], "sec": 1 - c} for s in (1, 2, 3)]):
        g = rcopy(gbuf.at[0], gbuf.at[i + 1], g_send.at[i], g_recv.at[i], dev)
        g.start()
        sends.append(g)
        gc.append(g)

    join(3)
    join(2)
    join(1)
    join(0)

    for g in gc:
        g.wait_recv()
    total = gbuf[0]
    for i in range(7):
        total = total + gbuf[i + 1]
    for k in range(2):
        acc = jnp.zeros((1, tr), F32)
        for d in range(4):
            v = total[2 * d : 2 * d + 1, :] + total[2 * d + 1 : 2 * d + 2, :]
            acc = acc + jnp.where(ids[k : k + 1, :] == ep[d], v, 0.0)
        gg_out[k : k + 1, :] = acc / gate[k : k + 1, :]

    for s in (1, 2, 3):
        qc[s].wait_recv()
    for k, out in ((0, comb_out), (1, grad_out)):
        v = keep[k]
        for s in (1, 2, 3):
            v = v + zr2[s, k].astype(F32)
        out[...] = v.astype(BF16)

    for d in sends:
        d.wait_send()


def fused(tokens, cotangent, expert_ids, gate_values, expand_weight, contract_weight):
    tr, wd = tokens.shape
    cap = 3 * tr // 4
    width, ff = expand_weight.shape[1:]
    rows = 4 * cap
    vm = pl.BlockSpec(memory_space=pltpu.VMEM)
    anyspace = pl.BlockSpec(memory_space=pl.ANY)
    dma = pltpu.SemaphoreType.DMA
    comb, grad, gg = pl.pallas_call(
        kernel,
        out_shape=(
            jax.ShapeDtypeStruct((tr, wd), BF16),
            jax.ShapeDtypeStruct((tr, wd), BF16),
            jax.ShapeDtypeStruct((2, tr), F32),
        ),
        in_specs=[vm, vm, vm, vm, anyspace, anyspace],
        out_specs=(vm, vm, vm),
        scratch_shapes=[
            pltpu.VMEM((width, ff), BF16),
            pltpu.VMEM((ff, width), BF16),
            pltpu.VMEM((4, 2, tr, wd), BF16),
            pltpu.VMEM((4, 4, 2, cap, wd), BF16),
            pltpu.VMEM((2, 4, 4, 2, cap, wd), BF16),
            pltpu.VMEM((4, cap, tr), BF16),
            pltpu.VMEM((4, cap, wd), F32),
            pltpu.VMEM((tr, rows), BF16),
            pltpu.VMEM((tr, rows), BF16),
            pltpu.VMEM((rows, ff), F32),
            pltpu.VMEM((rows, ff), F32),
            pltpu.VMEM((rows, ff), BF16),
            pltpu.VMEM((rows, ff), BF16),
            pltpu.VMEM((4, 2, rows, wd), F32),
            pltpu.VMEM((4, 2, rows, wd), BF16),
            pltpu.VMEM((4, 2, rows, wd), BF16),
            pltpu.VMEM((4, 4, 2, cap, wd), BF16),
            pltpu.VMEM((4, 4, 2, cap, wd), BF16),
            pltpu.VMEM((4, cap, 128), BF16),
            pltpu.VMEM((4, cap, 128), BF16),
            pltpu.VMEM((8, 8, tr), F32),
            pltpu.VMEM((4, 2, tr, wd), BF16),
            pltpu.VMEM((4, 2, tr, wd), BF16),
            pltpu.VMEM((2, tr, wd), F32),
            dma((2,)),
            dma((4,)), dma((4,)),
            dma((4, 4)), dma((4, 4)),
            dma((4,)), dma((4,)),
            dma((4,)), dma((4,)),
            dma((4, 4)), dma((4, 4)),
            dma((4,)), dma((4,)),
            dma((7,)), dma((7,)),
            dma((4,)), dma((4,)),
        ],
        compiler_params=pltpu.CompilerParams(
            collective_id=0, has_side_effects=True, vmem_limit_bytes=48 * 1024 * 1024
        ),
        cost_estimate=pl.CostEstimate(
            flops=8 * rows * width * ff, bytes_accessed=4 * width * ff, transcendentals=rows * ff
        ),
    )(tokens, cotangent, expert_ids.T, gate_values.T, expand_weight, contract_weight)
    return comb, grad, gg.T


gelu_coef = math.sqrt(2.0 / math.pi)
gelu_cubic = 0.044715


def gelu_parts(hidden):
    inner_arg = gelu_coef * (hidden + gelu_cubic * hidden * hidden * hidden)
    tanh_value = jnp.tanh(inner_arg)
    activation = 0.5 * hidden * (1.0 + tanh_value)
    derivative = 0.5 * (1.0 + tanh_value) + 0.5 * hidden * (
        1.0 - tanh_value * tanh_value
    ) * gelu_coef * (1.0 + 3.0 * gelu_cubic * hidden * hidden)
    return (activation, derivative)


def slot_positions(expert_ids, capacity):
    flat_ids = expert_ids.reshape(-1)
    place = jnp.arange(flat_ids.shape[0], dtype=jnp.int32)
    same = (flat_ids[:, None] == flat_ids[None, :]) & (place[None, :] < place[:, None])
    earlier = jnp.sum(same.astype(jnp.int32), axis=1)
    return flat_ids * capacity + earlier


def transposed_product(left, right):
    return lax.dot_general(
        left, right, (((1,), (1,)), ((), ())), preferred_element_type=jnp.float32
    )


def per_device(tokens, cotangent, expert_ids, gate_values, expand_weight, contract_weight):
    block_index = lax.axis_index("sec") * lax.axis_size("section") + lax.axis_index("section")
    tok_rows, width_share = tokens.shape
    experts = lax.axis_size("expert")
    capacity = 3 * tok_rows // experts
    slot_count = experts * capacity
    expand_local = expand_weight[0]
    contract_local = contract_weight[0]
    full_width = contract_local.shape[1]
    positions = slot_positions(expert_ids, capacity)
    placement_matrix = (
        positions[:, None] == jnp.arange(slot_count, dtype=jnp.int32)[None, :]
    ).astype(jnp.bfloat16)
    scaled_grad = (gate_values[:, :, None] * cotangent[:, None, :].astype(jnp.float32)).astype(
        jnp.bfloat16
    )

    def to_slots(pairs):
        return jnp.dot(placement_matrix.T, pairs, preferred_element_type=jnp.float32).astype(
            jnp.bfloat16
        )

    whole_tokens, whole_grad = (
        lax.all_gather(tokens, ("sec", "section"), axis=1, tiled=True),
        lax.all_gather(scaled_grad, ("sec", "section"), axis=2, tiled=True),
    )
    pair_tokens = jnp.broadcast_to(whole_tokens[:, None, :], (tok_rows, 2, full_width)).reshape(
        2 * tok_rows, full_width
    )
    send_x = to_slots(pair_tokens).reshape(experts, capacity, full_width)
    send_g = to_slots(whole_grad.reshape(2 * tok_rows, full_width)).reshape(
        experts, capacity, full_width
    )
    recv_x, recv_g = (
        lax.all_to_all(send_x, "expert", split_axis=0, concat_axis=0, tiled=True),
        lax.all_to_all(send_g, "expert", split_axis=0, concat_axis=0, tiled=True),
    )
    hidden = jnp.dot(
        recv_x.reshape(slot_count, full_width), expand_local, preferred_element_type=jnp.float32
    )
    grad_activation = transposed_product(recv_g.reshape(slot_count, full_width), contract_local)
    activation, derivative = gelu_parts(hidden)
    activation = activation.astype(jnp.bfloat16)
    grad_hidden = (grad_activation * derivative).astype(jnp.bfloat16)
    out_part = jnp.dot(activation, contract_local, preferred_element_type=jnp.float32).astype(
        jnp.bfloat16
    )
    back_part = transposed_product(grad_hidden, expand_local).astype(jnp.bfloat16)
    out_sum, back_sum = (
        lax.psum(out_part, ("sec", "section")).astype(jnp.float32),
        lax.psum(back_part, ("sec", "section")).astype(jnp.float32),
    )
    out_rows = out_sum.astype(jnp.bfloat16).reshape(experts, capacity, full_width)
    back_rows = back_sum.astype(jnp.bfloat16).reshape(experts, capacity, full_width)
    returned_out, returned_back = (
        lax.all_to_all(out_rows, "expert", split_axis=0, concat_axis=0, tiled=True),
        lax.all_to_all(back_rows, "expert", split_axis=0, concat_axis=0, tiled=True),
    )
    returned_out = lax.dynamic_slice_in_dim(returned_out, block_index * width_share, width_share, 2)
    returned_back = lax.dynamic_slice_in_dim(
        returned_back, block_index * width_share, width_share, 2
    )
    out_pairs = jnp.dot(
        placement_matrix,
        returned_out.reshape(slot_count, width_share),
        preferred_element_type=jnp.float32,
    ).reshape(tok_rows, 2, width_share)
    back_pairs = jnp.dot(
        placement_matrix,
        returned_back.reshape(slot_count, width_share),
        preferred_element_type=jnp.float32,
    ).reshape(tok_rows, 2, width_share)
    combined = jnp.sum(gate_values[:, :, None] * out_pairs, axis=1).astype(jnp.bfloat16)
    partial_dots = jnp.sum(cotangent[:, None, :].astype(jnp.float32) * out_pairs, axis=2)
    gate_grad = lax.psum(partial_dots, ("sec", "section"))
    input_grad = (back_pairs[:, 0, :] + back_pairs[:, 1, :]).astype(jnp.bfloat16)
    return (combined, input_grad, gate_grad)


def solution(mesh):
    small = dict(mesh.shape) == {"sec": 2, "section": 4, "expert": 4}
    return jax.shard_map(
        fused if small else per_device,
        mesh=mesh,
        in_specs=(
            P("expert", ("sec", "section")),
            P("expert", ("sec", "section")),
            P("expert", None),
            P("expert", None),
            P("expert", None, ("sec", "section")),
            P("expert", ("sec", "section"), None),
        ),
        out_specs=(
            P("expert", ("sec", "section")),
            P("expert", ("sec", "section")),
            P("expert", None),
        ),
        check_vma=False,
    )
```

```python
import math

import jax
import jax.numpy as jnp
from jax import lax
from jax.experimental import pallas as pl
from jax.experimental.pallas import tpu as pltpu
from jax.sharding import PartitionSpec as P

MESH = pl.DeviceIdType.MESH
F32 = jnp.float32
BF16 = jnp.bfloat16


def partners(i):
    return (i, i + 1 - 2 * lax.rem(i, 2), lax.rem(i + 2, 4), 3 - i)


def kernel(
    tok, cot, ids, gate, w1_hbm, w2_hbm,
    comb_out, grad_out, gg_out,
    w1, w2, zbuf, sendbuf, slots, pt, gslot, pmat, pgate, hid, gact, act, ghid,
    own, sibs, sibr, rsend, ret, xsend, xret, gbuf, zs2, zr2, keep,
    wsem, zsend, zrecv, asend, arecv, fsend, frecv, bsend, brecv,
    rs_send, rs_recv, x_send, x_recv, g_send, g_recv, q_send, q_recv,
):
    cap = slots.shape[4]
    wd = slots.shape[5]
    tr = tok.shape[0]
    rows = 4 * cap
    c = lax.axis_index("sec")
    z = lax.axis_index("section")
    e = lax.axis_index("expert")
    zp = partners(z)
    inner = (z * (3 - z)) // 2
    zq = (z, zp[1], inner * zp[3] + (1 - inner) * zp[2], inner * zp[2] + (1 - inner) * zp[3])
    ep = partners(e)

    def to_z(s):
        return {"section": zp[s]}

    def to_e(d):
        return {"expert": ep[d]}

    sib = {"sec": 1 - c}

    def rcopy(src, dst, ss, rs, dev):
        return pltpu.make_async_remote_copy(
            src_ref=src, dst_ref=dst, send_sem=ss, recv_sem=rs,
            device_id=dev, device_id_type=MESH,
        )

    cw1 = pltpu.make_async_copy(w1_hbm.at[0], w1, wsem.at[0])
    cw2 = pltpu.make_async_copy(w2_hbm.at[0], w2, wsem.at[1])
    cw1.start()
    cw2.start()

    zbuf[0, 0] = tok[...]
    zbuf[0, 1] = cot[...]
    barrier = pltpu.get_barrier_semaphore()
    peers = [to_z(s) for s in (1, 2, 3)] + [to_e(d) for d in (1, 2, 3)] + [sib]
    peers += [{"section": zp[s], "sec": 1 - c} for s in (1, 2, 3)]
    for p in peers:
        pl.semaphore_signal(barrier, inc=1, device_id=p, device_id_type=MESH)
    pl.semaphore_wait(barrier, len(peers))

    sends = []
    zc = {
        1: rcopy(zbuf.at[0], zbuf.at[1], zsend.at[1], zrecv.at[1], to_z(1)),
        2: rcopy(zbuf.at[0], zbuf.at[2], zsend.at[2], zrecv.at[2], to_z(3)),
        3: rcopy(zbuf.at[1], zbuf.at[3], zsend.at[3], zrecv.at[3], to_z(3)),
        4: rcopy(zbuf.at[2], zbuf.at[2], zsend.at[4], zrecv.at[2], to_z(1)),
        5: rcopy(zbuf.at[3], zbuf.at[3], zsend.at[5], zrecv.at[3], to_z(1)),
    }
    zc[1].start()
    sends.append(zc[1])

    def pass_on(i):
        @pl.when(inner == 1)
        def _():
            zc[i].start()

    pass_on(2)

    rid = lax.broadcasted_iota(jnp.int32, (8, tr), 0)
    erow = jnp.where(rid == 0, ep[0], jnp.where(rid == 1, ep[1], jnp.where(rid == 2, ep[2], jnp.where(rid == 3, ep[3], -1))))
    is0 = ids[0:1, :] == erow
    is1 = ids[1:2, :] == erow
    named = jnp.where(is0, 1.0, jnp.where(is1, 1.0, 0.0)).astype(F32)
    gates = jnp.where(is0, gate[0:1, :], jnp.where(is1, gate[1:2, :], 0.0))
    upper = (
        lax.broadcasted_iota(jnp.int32, (tr, tr), 0) < lax.broadcasted_iota(jnp.int32, (tr, tr), 1)
    ).astype(F32).astype(BF16)
    rank = jnp.dot(named.astype(BF16), upper, preferred_element_type=F32)
    key = jnp.where(named > 0.5, rank, -1.0).astype(jnp.int32)
    cid = lax.broadcasted_iota(jnp.int32, (cap, tr), 0)
    for d in range(4):
        hit = cid == key[d : d + 1, :]
        one = jnp.where(hit, 1.0, 0.0).astype(F32)
        weighed = jnp.where(hit, gates[d : d + 1, :], 0.0)
        pt[d] = one.astype(BF16)
        gslot[d] = jnp.broadcast_to(jnp.sum(weighed, axis=1, keepdims=True), (cap, wd))
        own[0, 0, d * cap : (d + 1) * cap, 0:tr] = one
        own[0, 1, d * cap : (d + 1) * cap, 0:tr] = weighed
    def block(core, zs):
        return pl.ds(pl.multiple_of((core * 4 + zs) * wd, wd), wd)

    def gather_step(half, core, s, first):
        if first:
            cw1.wait()
            cw2.wait()
        at = block(core, zq[s])
        xs = slots[half, s, :, 0].reshape(rows, wd)
        gs = slots[half, s, :, 1].reshape(rows, wd)
        hpart = jnp.dot(xs, w1[at, :], preferred_element_type=F32)
        gpart = lax.dot_general(gs, w2[:, at], (((1,), (1,)), ((), ())), preferred_element_type=F32)
        if first:
            hid[...] = hpart
            gact[...] = gpart
        else:
            hid[...] += hpart
            gact[...] += gpart

    ac = {}
    fc = {}

    def dispatch(s):
        if s:
            zc[s].wait_recv()
            pass_on(s + 2)
        xb = zbuf[s, 0]
        cb = zbuf[s, 1]
        for d in (1, 2, 3, 0):
            dst = slots.at[0, s, 0] if d == 0 else sendbuf.at[s, d]
            dst[0] = jnp.dot(pt[d], xb, preferred_element_type=F32).astype(BF16)
            dst[1] = (jnp.dot(pt[d], cb, preferred_element_type=F32) * gslot[d]).astype(BF16)
            if d:
                ac[s, d] = rcopy(sendbuf.at[s, d], slots.at[0, s, d], asend.at[s, d], arecv.at[s, d], to_e(d))
                ac[s, d].start()
                sends.append(ac[s, d])

    def take(s):
        for d in (1, 2, 3):
            ac[s, d].wait_recv()
        fc[s] = rcopy(slots.at[0, s], slots.at[1, s], fsend.at[s], frecv.at[s], sib)
        fc[s].start()
        sends.append(fc[s])
        gather_step(0, c, s, s == 0)

    def take_sib(s):
        fc[s].wait_recv()
        gather_step(1, 1 - c, s, False)

    dispatch(0)
    dispatch(1)
    pmat[...] = own[0, 0, :, 0:tr].T.astype(BF16)
    pgate[...] = own[0, 1, :, 0:tr].T.astype(BF16)
    dispatch(2)
    dispatch(3)
    take(0)
    take(1)
    take_sib(0)
    take(2)
    take_sib(1)
    take(3)
    take_sib(2)
    take_sib(3)

    coef = math.sqrt(2.0 / math.pi)
    cubic = 0.044715
    lane = lax.broadcasted_iota(jnp.int32, (cap, 128), 1)
    xc = {}
    for d in (1, 2, 3, 0):
        rr = slice(d * cap, (d + 1) * cap)
        h = hid[rr, :]
        ga = gact[rr, :]
        h2 = h * h
        u = jnp.tanh(coef * h * (1.0 + cubic * h2))
        half = 0.5 * (1.0 + u)
        a = (h * half).astype(BF16)
        act[rr, :] = a
        ghid[rr, :] = (ga * (half + 0.5 * h * (1.0 - u * u) * coef * (1.0 + 3.0 * cubic * h2))).astype(BF16)
        dots = jnp.sum(a.astype(F32) * ga, axis=1, keepdims=True)
        hi = dots.astype(BF16).astype(F32)
        lo = dots - hi
        extra = jnp.where(lane == 2 * d, hi, jnp.where(lane == 2 * d + 1, lo, 0.0)).astype(BF16)
        if d:
            xsend[d] = extra
            xc[d] = rcopy(xsend.at[d], xret.at[d], x_send.at[d], x_recv.at[d], to_e(d))
            xc[d].start()
            sends.append(xc[d])
        else:
            xret[0] = extra

    bc = {}
    rc = {}
    qc = {}

    def expand_back(s):
        for core, mine in ((1 - c, False), (c, True)):
            at = block(core, zp[s])
            o = jnp.dot(act[...], w2[:, at], preferred_element_type=F32)
            b = lax.dot_general(ghid[...], w1[at, :], (((1,), (1,)), ((), ())), preferred_element_type=F32)
            if mine:
                own[s, 0] = o
                own[s, 1] = b
            else:
                sibs[s, 0] = o.astype(BF16)
                sibs[s, 1] = b.astype(BF16)
                bc[s] = rcopy(sibs.at[s], sibr.at[s], bsend.at[s], brecv.at[s], sib)
                bc[s].start()
                sends.append(bc[s])

    def give_back(s):
        bc[s].wait_recv()
        for d in (1, 2, 3, 0):
            rr = slice(d * cap, (d + 1) * cap)
            dst = ret.at[s, 0] if d == 0 else rsend.at[s, d]
            for k in range(2):
                dst[k] = (own[s, k, rr, :] + sibr[s, k, rr, :].astype(F32)).astype(BF16)
            if d:
                rc[s, d] = rcopy(rsend.at[s, d], ret.at[s, d], rs_send.at[s, d], rs_recv.at[s, d], to_e(d))
                rc[s, d].start()
                sends.append(rc[s, d])

    def join(s):
        for d in (1, 2, 3):
            rc[s, d].wait_recv()
        o = jnp.dot(pgate[...], ret[s, :, 0].reshape(rows, wd), preferred_element_type=F32)
        b = jnp.dot(pmat[...], ret[s, :, 1].reshape(rows, wd), preferred_element_type=F32)
        if s:
            zs2[s, 0] = o.astype(BF16)
            zs2[s, 1] = b.astype(BF16)
            qc[s] = rcopy(zs2.at[s], zr2.at[s], q_send.at[s], q_recv.at[s], to_z(s))
            qc[s].start()
            sends.append(qc[s])
        else:
            keep[0] = o
            keep[1] = b

    expand_back(3)
    expand_back(2)
    give_back(3)
    expand_back(1)
    give_back(2)
    expand_back(0)
    give_back(1)
    give_back(0)

    for d in (1, 2, 3):
        xc[d].wait_recv()
    share = jnp.dot(pmat[...], xret[...].reshape(rows, 128), preferred_element_type=F32)
    gbuf[0] = share.T[0:8, :]
    gc = []
    for i, dev in enumerate([to_z(1), to_z(2), to_z(3), sib] + [{"section": zp[s], "sec": 1 - c} for s in (1, 2, 3)]):
        g = rcopy(gbuf.at[0], gbuf.at[i + 1], g_send.at[i], g_recv.at[i], dev)
        g.start()
        sends.append(g)
        gc.append(g)

    join(3)
    join(2)
    join(1)
    join(0)

    for g in gc:
        g.wait_recv()
    total = gbuf[0]
    for i in range(7):
        total = total + gbuf[i + 1]
    for k in range(2):
        acc = jnp.zeros((1, tr), F32)
        for d in range(4):
            v = total[2 * d : 2 * d + 1, :] + total[2 * d + 1 : 2 * d + 2, :]
            acc = acc + jnp.where(ids[k : k + 1, :] == ep[d], v, 0.0)
        gg_out[k : k + 1, :] = acc / gate[k : k + 1, :]

    for s in (1, 2, 3):
        qc[s].wait_recv()
    for k, out in ((0, comb_out), (1, grad_out)):
        v = keep[k]
        for s in (1, 2, 3):
            v = v + zr2[s, k].astype(F32)
        out[...] = v.astype(BF16)

    for d in sends:
        d.wait_send()

    @pl.when(inner == 1)
    def _():
        for i in (2, 3, 4, 5):
            zc[i].wait_send()


def fused(tokens, cotangent, expert_ids, gate_values, expand_weight, contract_weight):
    tr, wd = tokens.shape
    cap = 3 * tr // 4
    width, ff = expand_weight.shape[1:]
    rows = 4 * cap
    vm = pl.BlockSpec(memory_space=pltpu.VMEM)
    anyspace = pl.BlockSpec(memory_space=pltpu.HBM)
    dma = pltpu.SemaphoreType.DMA
    comb, grad, gg = pl.pallas_call(
        kernel,
        out_shape=(
            jax.ShapeDtypeStruct((tr, wd), BF16),
            jax.ShapeDtypeStruct((tr, wd), BF16),
            jax.ShapeDtypeStruct((2, tr), F32),
        ),
        in_specs=[vm, vm, vm, vm, anyspace, anyspace],
        out_specs=(vm, vm, vm),
        scratch_shapes=[
            pltpu.VMEM((width, ff), BF16),
            pltpu.VMEM((ff, width), BF16),
            pltpu.VMEM((4, 2, tr, wd), BF16),
            pltpu.VMEM((4, 4, 2, cap, wd), BF16),
            pltpu.VMEM((2, 4, 4, 2, cap, wd), BF16),
            pltpu.VMEM((4, cap, tr), BF16),
            pltpu.VMEM((4, cap, wd), F32),
            pltpu.VMEM((tr, rows), BF16),
            pltpu.VMEM((tr, rows), BF16),
            pltpu.VMEM((rows, ff), F32),
            pltpu.VMEM((rows, ff), F32),
            pltpu.VMEM((rows, ff), BF16),
            pltpu.VMEM((rows, ff), BF16),
            pltpu.VMEM((4, 2, rows, wd), F32),
            pltpu.VMEM((4, 2, rows, wd), BF16),
            pltpu.VMEM((4, 2, rows, wd), BF16),
            pltpu.VMEM((4, 4, 2, cap, wd), BF16),
            pltpu.VMEM((4, 4, 2, cap, wd), BF16),
            pltpu.VMEM((4, cap, 128), BF16),
            pltpu.VMEM((4, cap, 128), BF16),
            pltpu.VMEM((8, 8, tr), F32),
            pltpu.VMEM((4, 2, tr, wd), BF16),
            pltpu.VMEM((4, 2, tr, wd), BF16),
            pltpu.VMEM((2, tr, wd), F32),
            dma((2,)),
            dma((6,)), dma((4,)),
            dma((4, 4)), dma((4, 4)),
            dma((4,)), dma((4,)),
            dma((4,)), dma((4,)),
            dma((4, 4)), dma((4, 4)),
            dma((4,)), dma((4,)),
            dma((7,)), dma((7,)),
            dma((4,)), dma((4,)),
        ],
        compiler_params=pltpu.CompilerParams(
            collective_id=0, has_side_effects=True, vmem_limit_bytes=48 * 1024 * 1024
        ),
        cost_estimate=pl.CostEstimate(
            flops=8 * rows * width * ff, bytes_accessed=4 * width * ff, transcendentals=rows * ff
        ),
    )(tokens, cotangent, expert_ids.T, gate_values.T, expand_weight, contract_weight)
    return comb, grad, gg.T


gelu_coef = math.sqrt(2.0 / math.pi)
gelu_cubic = 0.044715


def gelu_parts(hidden):
    inner_arg = gelu_coef * (hidden + gelu_cubic * hidden * hidden * hidden)
    tanh_value = jnp.tanh(inner_arg)
    activation = 0.5 * hidden * (1.0 + tanh_value)
    derivative = 0.5 * (1.0 + tanh_value) + 0.5 * hidden * (
        1.0 - tanh_value * tanh_value
    ) * gelu_coef * (1.0 + 3.0 * gelu_cubic * hidden * hidden)
    return (activation, derivative)


def slot_positions(expert_ids, capacity):
    flat_ids = expert_ids.reshape(-1)
    place = jnp.arange(flat_ids.shape[0], dtype=jnp.int32)
    same = (flat_ids[:, None] == flat_ids[None, :]) & (place[None, :] < place[:, None])
    earlier = jnp.sum(same.astype(jnp.int32), axis=1)
    return flat_ids * capacity + earlier


def transposed_product(left, right):
    return lax.dot_general(
        left, right, (((1,), (1,)), ((), ())), preferred_element_type=jnp.float32
    )


def per_device(tokens, cotangent, expert_ids, gate_values, expand_weight, contract_weight):
    block_index = lax.axis_index("sec") * lax.axis_size("section") + lax.axis_index("section")
    tok_rows, width_share = tokens.shape
    experts = lax.axis_size("expert")
    capacity = 3 * tok_rows // experts
    slot_count = experts * capacity
    expand_local = expand_weight[0]
    contract_local = contract_weight[0]
    full_width = contract_local.shape[1]
    positions = slot_positions(expert_ids, capacity)
    placement_matrix = (
        positions[:, None] == jnp.arange(slot_count, dtype=jnp.int32)[None, :]
    ).astype(jnp.bfloat16)
    scaled_grad = (gate_values[:, :, None] * cotangent[:, None, :].astype(jnp.float32)).astype(
        jnp.bfloat16
    )

    def to_slots(pairs):
        return jnp.dot(placement_matrix.T, pairs, preferred_element_type=jnp.float32).astype(
            jnp.bfloat16
        )

    whole_tokens, whole_grad = (
        lax.all_gather(tokens, ("sec", "section"), axis=1, tiled=True),
        lax.all_gather(scaled_grad, ("sec", "section"), axis=2, tiled=True),
    )
    pair_tokens = jnp.broadcast_to(whole_tokens[:, None, :], (tok_rows, 2, full_width)).reshape(
        2 * tok_rows, full_width
    )
    send_x = to_slots(pair_tokens).reshape(experts, capacity, full_width)
    send_g = to_slots(whole_grad.reshape(2 * tok_rows, full_width)).reshape(
        experts, capacity, full_width
    )
    recv_x, recv_g = (
        lax.all_to_all(send_x, "expert", split_axis=0, concat_axis=0, tiled=True),
        lax.all_to_all(send_g, "expert", split_axis=0, concat_axis=0, tiled=True),
    )
    hidden = jnp.dot(
        recv_x.reshape(slot_count, full_width), expand_local, preferred_element_type=jnp.float32
    )
    grad_activation = transposed_product(recv_g.reshape(slot_count, full_width), contract_local)
    activation, derivative = gelu_parts(hidden)
    activation = activation.astype(jnp.bfloat16)
    grad_hidden = (grad_activation * derivative).astype(jnp.bfloat16)
    out_part = jnp.dot(activation, contract_local, preferred_element_type=jnp.float32).astype(
        jnp.bfloat16
    )
    back_part = transposed_product(grad_hidden, expand_local).astype(jnp.bfloat16)
    out_sum, back_sum = (
        lax.psum(out_part, ("sec", "section")).astype(jnp.float32),
        lax.psum(back_part, ("sec", "section")).astype(jnp.float32),
    )
    out_rows = out_sum.astype(jnp.bfloat16).reshape(experts, capacity, full_width)
    back_rows = back_sum.astype(jnp.bfloat16).reshape(experts, capacity, full_width)
    returned_out, returned_back = (
        lax.all_to_all(out_rows, "expert", split_axis=0, concat_axis=0, tiled=True),
        lax.all_to_all(back_rows, "expert", split_axis=0, concat_axis=0, tiled=True),
    )
    returned_out = lax.dynamic_slice_in_dim(returned_out, block_index * width_share, width_share, 2)
    returned_back = lax.dynamic_slice_in_dim(
        returned_back, block_index * width_share, width_share, 2
    )
    out_pairs = jnp.dot(
        placement_matrix,
        returned_out.reshape(slot_count, width_share),
        preferred_element_type=jnp.float32,
    ).reshape(tok_rows, 2, width_share)
    back_pairs = jnp.dot(
        placement_matrix,
        returned_back.reshape(slot_count, width_share),
        preferred_element_type=jnp.float32,
    ).reshape(tok_rows, 2, width_share)
    combined = jnp.sum(gate_values[:, :, None] * out_pairs, axis=1).astype(jnp.bfloat16)
    partial_dots = jnp.sum(cotangent[:, None, :].astype(jnp.float32) * out_pairs, axis=2)
    gate_grad = lax.psum(partial_dots, ("sec", "section"))
    input_grad = (back_pairs[:, 0, :] + back_pairs[:, 1, :]).astype(jnp.bfloat16)
    return (combined, input_grad, gate_grad)


def solution(mesh):
    small = dict(mesh.shape) == {"sec": 2, "section": 4, "expert": 4}
    return jax.shard_map(
        fused if small else per_device,
        mesh=mesh,
        in_specs=(
            P("expert", ("sec", "section")),
            P("expert", ("sec", "section")),
            P("expert", None),
            P("expert", None),
            P("expert", None, ("sec", "section")),
            P("expert", ("sec", "section"), None),
        ),
        out_specs=(
            P("expert", ("sec", "section")),
            P("expert", ("sec", "section")),
            P("expert", None),
        ),
        check_vma=False,
    )
```
